512 devices in a mesh: mode: 8 (over y_lo, x), slab: 64 (over z, y_hi, core).
Axes of the slice: x: 4, y: 4 (y_hi: 2, y_lo: 2; y = y_hi * 2 + y_lo), z: 16, core: 2. Of those that a mesh axis runs over, the one named last changes fastest.
Arguments:
- chaos_field: float32 [1024, 192, 1024], P('mode', 'slab'), may hold values from -4 to 4
- diffusivity: float32 [192, 1024], P('slab'), may hold values from 0.03 to 0.16
- growth_rate: float32 [192, 1024], P('slab'), may hold values from 0.3 to 3
- mode_table: int32 [1024, 8], replicated, may hold values from 0 to 2, as said below
- point_index: int32 [2048, 8], replicated, may hold values from 0 to 6
Outputs:
- final_field: float32 [1024, 192, 1024], P('mode', 'slab')
The draws below stay inside these ranges and needn't reach their ends.
Inputs may be any that keep to these rules, and one draw needn't show every extreme that they name: `mode_table`: the rows are distinct multi-indices.
All inputs are finite; a program needn't handle non-finite values.
Results may differ from the reference program's by a relative error of at most 0.0035.
Values may be sent and summed in bfloat16 or wider, within the bound.
A program may use at most 64 MiB of HBM per device.

```python
import math
import jax
import jax.numpy as jnp
from jax import lax

MODES = 1024
POINTS = 2048
DIMS = 8
NODES = 7
NX = 32
NY = 32
PLANES_DEV = 3
SWEEPS = 3
STEPS = 2
PLANES = 192
N_SLAB = 64


def draw_mode_table(key, part):
    chosen = jax.random.permutation(jax.random.fold_in(key, 17), 3 ** DIMS)[:MODES]
    digits = [chosen // 3 ** place % 3 for place in range(DIMS)]
    return jnp.stack(digits, axis=1).astype(jnp.int32)


def draw_chaos_field(key, part):
    shape = (MODES, PLANES, NX * NY)
    field_key = jax.random.fold_in(key, 41)
    result = jnp.clip(jax.random.normal(field_key, shape, jnp.float32), -4.0, 4.0)
    return result.astype(jnp.float32)


def place_ends(array, key, smallest, high):
    spot = [jax.random.randint(jax.random.fold_in(key, axis), (), 0, length) for axis, length in enumerate(array.shape)]
    longest = array.shape.index(max(array.shape))
    next_to = spot[:longest] + [(spot[longest] + 1) % array.shape[longest]] + spot[longest + 1:]
    return array.at[tuple(spot)].set(smallest).at[tuple(next_to)].set(high)


def block_levels(key, shape, cuts, smallest, top_value):
    loudness, own = 1.0, jax.random.fold_in(key, 6)
    for dim, parts in cuts:
        draws = jnp.exp(jax.random.uniform(jax.random.fold_in(own, dim), (parts,), jnp.float32, smallest / len(cuts), top_value / len(cuts)))
        loudness = loudness * jnp.repeat(draws, shape[dim] // parts).reshape([-1 if axis == dim else 1 for axis in range(len(shape))])
    return loudness


def setup_inputs(seed: int = 0) -> dict:
    key_list = jax.random.split(jax.random.key(seed), 6)
    chaos_field = draw_chaos_field(jax.random.fold_in(key_list[5], 71), 0)
    diffusivity = jnp.clip(jnp.exp(math.log(0.16) - 1.6739764 * jax.random.uniform(key_list[1], (PLANES, NX * NY), jnp.float32) ** block_levels(key_list[1], (PLANES, NX * NY), ((0, 64),), -0.2, 0.2)), 0.03, 0.16)
    growth_rate = jnp.clip(jnp.exp(math.log(3.0) - 2.3025851 * jax.random.uniform(key_list[2], (PLANES, NX * NY), jnp.float32) ** block_levels(key_list[2], (PLANES, NX * NY), ((0, 64),), -0.2, 0.2)), 0.3, 3.0)
    mode_table = draw_mode_table(jax.random.fold_in(key_list[5], 71), 0)
    point_index = place_ends(jax.random.randint(key_list[4], (POINTS, DIMS), 0, NODES), jax.random.fold_in(key_list[4], 1), 0, NODES - 1).astype(jnp.int32)
    return {"chaos_field": chaos_field, "diffusivity": diffusivity, "growth_rate": growth_rate, "mode_table": mode_table, "point_index": point_index}


def make_basis(mode_table, point_index):
    abscissa = (point_index.astype(jnp.float32) - (NODES - 1) / 2.0) * 0.32
    second = (abscissa * abscissa - 1.0) * 0.7071067811865476
    result = None
    for place in range(mode_table.shape[1]):
        degree = mode_table[None, :, place]
        factor = jnp.where(degree == 0, jnp.float32(1.0), jnp.where(degree == 1, abscissa[:, place:place + 1], second[:, place:place + 1]))
        result = factor if result is None else result * factor
    return result


def sweep(extended, kappa_mid, size_x, size_y):
    middle = extended[:, 1:-1]
    cell_count = middle.shape[2]
    column = lax.broadcasted_iota(jnp.int32, (1, 1, cell_count), 2) % size_y
    x_pair = jnp.roll(middle, size_y, 2) + jnp.roll(middle, -size_y, 2)
    y_lower = jnp.where(column == 0, jnp.roll(middle, 1 - size_y, 2), jnp.roll(middle, 1, 2))
    y_upper = jnp.where(column == size_y - 1, jnp.roll(middle, size_y - 1, 2), jnp.roll(middle, -1, 2))
    beside_all = x_pair + (y_lower + y_upper)
    beside_all = beside_all + extended[:, 2:] + extended[:, :-2]
    return middle + kappa_mid[None] * (beside_all - 6.0 * middle)


def reference(chaos_field, diffusivity, growth_rate, mode_table, point_index):
    basis_low = make_basis(mode_table, point_index).astype(jnp.bfloat16)
    basis_wide = lax.optimization_barrier(basis_low).astype(jnp.float32)
    forward_scale = 8.0 * MODES ** -0.5
    backward_scale = 1.4 * MODES ** 0.5 / POINTS
    current = chaos_field
    total_modes, total_planes, cell_count = chaos_field.shape
    block_cells = PLANES_DEV * cell_count
    growth_blocks = growth_rate.reshape(N_SLAB, block_cells)

    def react_block(pair):
        block_field, block_growth = pair
        low = lax.optimization_barrier(block_field.astype(jnp.bfloat16)).astype(jnp.float32)
        values = jnp.dot(basis_wide, low, precision=lax.Precision.HIGHEST) * forward_scale
        reaction = (0.5 * (block_growth[None] * values - values * values * values)).astype(jnp.bfloat16)
        reaction = lax.optimization_barrier(reaction).astype(jnp.float32)
        return jnp.dot(basis_wide.T, reaction, precision=lax.Precision.HIGHEST) * backward_scale

    for outer_step in range(STEPS):
        for sweep_step in range(SWEEPS):
            extended = jnp.pad(current, ((0, 0), (1, 1), (0, 0)))
            current = sweep(extended, diffusivity, NX, NY)
        blocked = current.reshape(total_modes, N_SLAB, block_cells).transpose(1, 0, 2)
        increment = lax.map(react_block, (blocked, growth_blocks))
        increment = increment.transpose(1, 0, 2).reshape(total_modes, total_planes, cell_count)
        current = current + increment
    return current
```

```python
import functools
import jax
import jax.numpy as jnp
from jax import lax
from jax.experimental import pallas as pl
from jax.experimental.pallas import tpu as pltpu
from jax.sharding import PartitionSpec as P

MESH = pl.DeviceIdType.MESH
F32, BF16, I16, I32 = jnp.float32, jnp.bfloat16, jnp.int16, jnp.int32
MODES = 1024
POINTS = 2048
SWEEPS = 3
L = 128
GROUPS = MODES // L
ROWS = 384
HALF = ROWS // 2
NCH = 4
GPC = GROUPS // NCH
FACES = (48, 48, 48, 48, 64, 64)
OFFS = (0, 48, 96, 144, 192, 256)
FROWS = 320
STEP = 32000.0
INV_LN2 = 1.4426950408889634


def kernel(
    x_hbm, dif_hbm, gro_hbm, mt_hbm, pi_hbm, out_hbm,
    xs, kg_src, mt, pi, tr, snd, rcv, kg_rcv, kap, gro, cellmap,
    fld, fsnd, frcv, basis, low, react, fin, fin_rcv,
    in_sem, a_send, a_recv, kg_send, kg_recv, h_send, h_recv, f_send, f_recv, out_sem,
):
    m, s = lax.axis_index("mode"), lax.axis_index("slab")
    depth = lax.axis_size("slab") // 4
    cx, ylo = m % 4, m // 4
    core, yhi, cz = s % 2, (s // 2) % 2, s // 4
    cy = yhi * 2 + ylo

    def at(x, y, z, c):
        return ((y % 2) * 4 + x, z * 4 + (y // 2) * 2 + c)

    loads = [pltpu.make_async_copy(x_hbm.at[p], xs.at[p], in_sem.at[p]) for p in range(3)]
    loads.append(pltpu.make_async_copy(dif_hbm, kg_src.at[0], in_sem.at[3]))
    loads.append(pltpu.make_async_copy(gro_hbm, kg_src.at[1], in_sem.at[4]))
    loads.append(pltpu.make_async_copy(mt_hbm, mt, in_sem.at[5]))
    loads.append(pltpu.make_async_copy(pi_hbm, pi, in_sem.at[6]))
    for c in loads:
        c.start()

    zup_z = jnp.where(core == 1, (cz + 1) % depth, cz)
    zdn_z = jnp.where(core == 0, (cz + depth - 1) % depth, cz)
    up = at(cx, cy, zup_z, 1 - core)
    down = at(cx, cy, zdn_z, 1 - core)
    partners = (
        at((cx + 1) % 4, cy, cz, core),
        at((cx + 3) % 4, cy, cz, core),
        at(cx, (cy + 1) % 4, cz, core),
        at(cx, (cy + 3) % 4, cz, core),
        up,
        down,
    )

    barrier = pltpu.get_barrier_semaphore()
    place = (cy * 4 + cx) * 2 + core

    def greet(k, carry):
        q = (place + k) % 32
        pl.semaphore_signal(
            barrier, inc=1, device_id=at((q // 2) % 4, q // 8, cz, q % 2), device_id_type=MESH
        )
        return carry

    lax.fori_loop(1, 32, greet, 0)
    far_z = jnp.where(core == 1, zup_z, zdn_z)
    pl.semaphore_signal(
        barrier, inc=1, device_id=at(cx, cy, far_z, 1 - core), device_id_type=MESH
    )

    big = jnp.zeros((8, L), F32)
    for p in range(3):
        loads[p].wait()

        def turn(b, big, p=p):
            block = jnp.transpose(xs[p, :, pl.ds(pl.multiple_of(b * L, L), L)])
            tr[pl.ds(pl.multiple_of((p * 8 + b) * L, L), L), :] = block
            for i in range(16):
                big = jnp.maximum(big, jnp.abs(block[8 * i : 8 * i + 8]))
            return big

        big = lax.fori_loop(0, 8, turn, big)
    top = jnp.maximum(jnp.max(big, axis=0, keepdims=True), 1e-30)
    level = jnp.ceil(jnp.log(top) * INV_LN2)
    gain = jnp.exp2(-level) * STEP

    tag = jnp.broadcast_to(level, (16, L)).astype(I32).astype(I16)
    for d in range(16):
        snd[d, HALF : HALF + 16, :] = tag

    def code(i, carry):
        p, b = i // 8, i % 8
        for y in range(4):
            parts = [
                tr[pl.ds(pl.multiple_of(i * L + xi * 32 + y * 8, 8), 8), :] for xi in range(4)
            ]
            tile = jnp.round(jnp.concatenate(parts, axis=0) * gain).astype(I32).astype(I16)
            row = pl.multiple_of(p * 64 + (b % 2) * 32, 32)
            snd[y * 4 + b // 2, pl.ds(row, 32), :] = tile
        return carry

    lax.fori_loop(0, 24, code, 0)

    pl.semaphore_wait(barrier, 32)

    def spread(k, wait):
        px, py = (cx + k) % 4, (cy + k // 4) % 4
        return pltpu.make_async_remote_copy(
            src_ref=snd.at[py * 4 + px],
            dst_ref=rcv.at[m * 2 + core],
            send_sem=a_send.at[k],
            recv_sem=a_recv.at[m * 2 + core],
            device_id=at(px, py, cz, yhi),
            device_id_type=MESH,
        )

    own = pltpu.make_async_copy(snd.at[cy * 4 + cx], rcv.at[m * 2 + core], a_recv.at[m * 2 + core])

    @pl.when(core == yhi)
    def _():
        own.start()

    @pl.when(core != yhi)
    def _():
        spread(0, None).start()

    def spread_start(k, carry):
        spread(k, None).start()
        return carry

    lax.fori_loop(1, 16, spread_start, 0)

    loads[3].wait()
    loads[4].wait()

    def coeff(h):
        return pltpu.make_async_remote_copy(
            src_ref=kg_src,
            dst_ref=kg_rcv.at[core],
            send_sem=kg_send.at[h],
            recv_sem=kg_recv.at[core],
            device_id=(m, cz * 4 + h * 2 + yhi),
            device_id_type=MESH,
        )

    kg_own = pltpu.make_async_copy(kg_src, kg_rcv.at[core], kg_recv.at[core])

    @pl.when(core == yhi)
    def _():
        kg_own.start()
        coeff(1 - yhi).start()

    @pl.when(core != yhi)
    def _():
        coeff(yhi).start()
        coeff(1 - yhi).start()

    loads[5].wait()
    loads[6].wait()
    k8 = lax.broadcasted_iota(I32, (8, 8), 1)
    r8 = lax.broadcasted_iota(I32, (8, 8), 0)
    power = jnp.where(
        k8 % 4 == 0, 1.0, jnp.where(k8 % 4 == 1, 3.0, jnp.where(k8 % 4 == 2, 9.0, 27.0))
    )
    weight = jnp.where(k8 // 4 == r8, power, 0.0).astype(BF16)
    codes = lax.dot_general(
        weight, mt[...].astype(F32).astype(BF16), (((1,), (1,)), ((), ())),
        preferred_element_type=F32,
    )
    hot_row = lax.broadcasted_iota(I32, (256, MODES), 0)
    hot_key = jnp.where(hot_row < 243, hot_row % 81, -1).astype(F32)
    hots = [
        jnp.where(hot_key == codes[j : j + 1, :], 1.0, 0.0).astype(BF16) for j in range(2)
    ]
    lane = lax.broadcasted_iota(I32, (8, 256), 1)
    combo = lane % 81
    digits = [(combo // 3**j) % 3 for j in range(4)]
    third = lane // 81
    QB = 64

    def build(i, carry):
        base = pl.multiple_of(i * QB, QB)
        picked = []
        for j in range(2):
            tiles = []
            for t in range(QB // 8):
                node = pi[pl.ds(base + t * 8, 8), :].astype(F32)
                first = (node - 3.0) * 0.32
                result = None
                for d in range(4):
                    h1 = jnp.broadcast_to(first[:, j * 4 + d : j * 4 + d + 1], (8, 256))
                    h2 = (h1 * h1 - 1.0) * 0.7071067811865476
                    factor = jnp.where(digits[d] == 0, 1.0, jnp.where(digits[d] == 1, h1, h2))
                    result = factor if result is None else result * factor
                high = result.astype(BF16).astype(F32)
                rest = result - high
                mid = rest.astype(BF16).astype(F32)
                tail = rest - mid
                tiles.append(jnp.where(third == 0, high, jnp.where(third == 1, mid, tail)))
            table = jnp.concatenate(tiles, axis=0).astype(BF16)
            picked.append(jnp.dot(table, hots[j], preferred_element_type=F32))
        basis[pl.ds(base, QB), :] = (picked[0] * picked[1]).astype(BF16)
        return carry

    lax.fori_loop(0, POINTS // QB, build, 0)

    for c in range(2):
        pltpu.make_async_copy(kg_rcv.at[c], kg_rcv.at[c], kg_recv.at[c]).wait()
    for c in range(2):
        for b in range(2):
            cols = pl.ds(pl.multiple_of(cx * 256 + b * L, L), L)
            rows8 = [kg_rcv[c, 0, :, cols], kg_rcv[c, 1, :, cols], jnp.zeros((L - 6, L), F32)]
            cellmap[...] = jnp.transpose(jnp.concatenate(rows8, axis=0))
            for xi in range(4):
                tile = cellmap[pl.ds(pl.multiple_of(xi * 32 + cy * 8, 8), 8), :]
                for p in range(3):
                    to = (c * 3 + p) * 64 + (b * 4 + xi) * 8
                    kap[to : to + 8, :] = jnp.broadcast_to(tile[:, p : p + 1], (8, L))
                    gro[to : to + 8, :] = jnp.broadcast_to(tile[:, 3 + p : 4 + p], (8, L)) * 0.125

    def face_copies(sw, ch):
        out = []
        for f in range(6):
            rows = pl.ds(OFFS[f] * GPC, FACES[f] * GPC)
            out.append(
                pltpu.make_async_remote_copy(
                    src_ref=fsnd.at[sw, ch, rows],
                    dst_ref=frcv.at[sw, ch, rows],
                    send_sem=h_send.at[sw],
                    recv_sem=h_recv.at[sw, ch],
                    device_id=partners[f],
                    device_id_type=MESH,
                )
            )
        return out

    def send_faces(sw, par, ch):
        def fill(gg, carry):
            g = ch * GPC + gg

            def put(f, value):
                row = pl.multiple_of(OFFS[f] * GPC + gg * FACES[f], 16)
                fsnd[sw, ch, pl.ds(row, FACES[f]), :] = value.astype(BF16)

            put(0, jnp.concatenate([fld[par, g, z * 64 + 56 : z * 64 + 64, :] for z in range(6)], 0))
            put(1, jnp.concatenate([fld[par, g, z * 64 : z * 64 + 8, :] for z in range(6)], 0))
            put(2, jnp.concatenate([fld[par, g, pl.ds(z * 64 + 7, 8, stride=8), :] for z in range(6)], 0))
            put(3, jnp.concatenate([fld[par, g, pl.ds(z * 64, 8, stride=8), :] for z in range(6)], 0))
            put(4, fld[par, g, 320:384, :])
            put(5, fld[par, g, 0:64, :])
            return carry

        lax.fori_loop(0, GPC, fill, 0)
        for c in face_copies(sw, ch):
            c.start()

    first_plane = jnp.logical_and(cz == 0, core == 0)
    last_plane = jnp.logical_and(cz == depth - 1, core == 1)
    sub = lax.broadcasted_iota(I32, (8, L), 0)

    def sweep(sw, ch):
        par = sw % 2
        pltpu.make_async_copy(frcv.at[sw, ch], frcv.at[sw, ch], h_recv.at[sw, ch]).wait()

        def group(gg, carry):
            g = ch * GPC + gg

            def halo(f):
                row = pl.multiple_of(OFFS[f] * GPC + gg * FACES[f], 16)
                return frcv[sw, ch, pl.ds(row, FACES[f]), :].astype(F32)

            xl, xh, yl, yh = halo(0), halo(1), halo(2), halo(3)
            zl = jnp.where(first_plane, 0.0, halo(4))
            zh = jnp.where(last_plane, 0.0, halo(5))
            for z in range(6):
                for x in range(8):
                    r = z * 64 + x * 8
                    mid = fld[par, g, r : r + 8, :]
                    xm = fld[par, g, r - 8 : r, :] if x else xl[z * 8 : z * 8 + 8]
                    xp = fld[par, g, r + 8 : r + 16, :] if x < 7 else xh[z * 8 : z * 8 + 8]
                    zm = fld[par, g, r - 64 : r - 56, :] if z else zl[x * 8 : x * 8 + 8]
                    zp = fld[par, g, r + 64 : r + 72, :] if z < 5 else zh[x * 8 : x * 8 + 8]
                    e = z * 8 + x
                    ym = jnp.where(sub == 0, yl[e : e + 1], pltpu.roll(mid, 1, 0))
                    yp = jnp.where(sub == 7, yh[e : e + 1], pltpu.roll(mid, 7, 0))
                    total = ((xm + xp) + (ym + yp)) + (zp + zm)
                    fld[1 - par, g, r : r + 8, :] = mid + kap[r : r + 8, :] * (total - 6.0 * mid)
            return carry

        lax.fori_loop(0, GPC, group, 0)

    def lower(par, ch):
        for gg in range(GPC):
            col = pl.ds(pl.multiple_of((ch * GPC + gg) * L, L), L)
            low[:, col] = fld[par, ch * GPC + gg].astype(BF16)

    def diffuse(first_sweep):
        def one(i, carry):
            t, ch = i // NCH, i % NCH
            sw = first_sweep + t
            sweep(sw, ch)

            @pl.when(t < SWEEPS - 1)
            def _():
                send_faces(sw + 1, (sw + 1) % 2, ch)

            @pl.when(t == SWEEPS - 1)
            def _():
                lower((sw + 1) % 2, ch)

            return carry

        lax.fori_loop(0, SWEEPS * NCH, one, 0)

    QC = 256

    def forward(i, carry):
        at_q = pl.ds(pl.multiple_of(i * QC, QC), QC)
        v = lax.dot_general(
            low[...], basis[at_q, :], (((1,), (1,)), ((), ())), preferred_element_type=F32
        )
        rate = jnp.concatenate([gro[...]] * (QC // L), axis=1)
        react[:, at_q] = (v * (rate - (v * v) * (1.0 / 128.0))).astype(BF16)
        return carry

    def increment(ch):
        cols = pl.ds(pl.multiple_of(ch * GPC * L, GPC * L), GPC * L)
        inc = jnp.dot(react[...], basis[:, cols], preferred_element_type=F32)
        return inc * (1.4 * MODES**0.5 / POINTS)

    def arrive(ch, carry):
        def one(gg, carry):
            g = ch * GPC + gg
            for c in range(2):
                slot = g * 2 + c
                pltpu.make_async_copy(rcv.at[slot], rcv.at[slot], a_recv.at[slot]).wait()
                level = rcv[slot, HALF : HALF + 16, :].astype(I32).astype(F32)[0:1]
                unit = jnp.exp2(level) * (1.0 / STEP)
                fld[0, g, c * HALF : (c + 1) * HALF, :] = (
                    rcv[slot, 0:HALF, :].astype(I32).astype(F32) * unit
                )
            return carry

        lax.fori_loop(0, GPC, one, 0)
        send_faces(0, 0, ch)
        return carry

    lax.fori_loop(0, NCH, arrive, 0)

    diffuse(0)
    lax.fori_loop(0, POINTS // QC, forward, 0)

    def back(ch, carry):
        inc = increment(ch)
        for gg in range(GPC):
            fld[1, ch * GPC + gg] += inc[:, gg * L : (gg + 1) * L]
        send_faces(SWEEPS, 1, ch)
        return carry

    lax.fori_loop(0, NCH, back, 0)
    diffuse(SWEEPS)
    lax.fori_loop(0, POINTS // QC, forward, 0)

    patch = cy * 4 + cx

    def home(g, c):
        return pltpu.make_async_remote_copy(
            src_ref=fin.at[g * 2 + c],
            dst_ref=fin_rcv.at[patch],
            send_sem=f_send.at[g * 2 + c],
            recv_sem=f_recv.at[patch],
            device_id=(g, cz * 4 + core * 2 + c),
            device_id_type=MESH,
        )

    def stays(g, c):
        return pltpu.make_async_copy(fin.at[g * 2 + c], fin_rcv.at[patch], f_recv.at[patch])

    def is_own(g, c):
        return jnp.logical_and(g == m, jnp.logical_and(core == yhi, c == core))

    def finish(ch, carry):
        inc = increment(ch)
        for gg in range(GPC):
            g = ch * GPC + gg
            done = (fld[0, g] + inc[:, gg * L : (gg + 1) * L]).astype(BF16)
            for c in range(2):
                fin[g * 2 + c] = done[c * HALF : (c + 1) * HALF]

                @pl.when(is_own(g, c))
                def _():
                    stays(g, c).start()

                @pl.when(jnp.logical_not(is_own(g, c)))
                def _():
                    home(g, c).start()

        return carry

    lax.fori_loop(0, NCH, finish, 0)

    def collect(i, carry):
        pltpu.make_async_copy(fin_rcv.at[i], fin_rcv.at[i], f_recv.at[i]).wait()
        return carry

    lax.fori_loop(0, 16, collect, 0)
    stores = [pltpu.make_async_copy(xs.at[p], out_hbm.at[p], out_sem.at[p]) for p in range(3)]
    for p in range(3):

        def unturn(b, carry, p=p):
            row = pl.multiple_of(p * 64 + (b % 2) * 32, 32)
            patches = [
                fin_rcv[y * 4 + b // 2, pl.ds(row, 32), :].astype(F32) for y in range(4)
            ]
            block = jnp.concatenate(
                [patches[y][xi * 8 : xi * 8 + 8] for xi in range(4) for y in range(4)], axis=0
            )
            xs[p, :, pl.ds(pl.multiple_of(b * L, L), L)] = jnp.transpose(block)
            return carry

        lax.fori_loop(0, 8, unturn, 0)
        stores[p].start()

    @pl.when(core != yhi)
    def _():
        spread(0, None).wait_send()
        coeff(yhi).wait_send()
        coeff(1 - yhi).wait_send()

    @pl.when(core == yhi)
    def _():
        coeff(1 - yhi).wait_send()

    def spread_done(k, carry):
        spread(k, None).wait_send()
        return carry

    lax.fori_loop(1, 16, spread_done, 0)

    def faces_done(sw, carry):
        pltpu.make_async_copy(fsnd.at[sw], fsnd.at[sw], h_send.at[sw]).wait()
        return carry

    lax.fori_loop(0, 2 * SWEEPS, faces_done, 0)

    def home_done(i, carry):
        g, c = i // 2, i % 2

        @pl.when(jnp.logical_not(is_own(g, c)))
        def _():
            home(g, c).wait_send()

        return carry

    lax.fori_loop(0, 16, home_done, 0)
    for p in range(3):
        stores[p].wait()


def per_device(chaos_field, diffusivity, growth_rate, mode_table, point_index):
    any_spec = pl.BlockSpec(memory_space=pl.ANY)
    V = pltpu.VMEM
    DMA = pltpu.SemaphoreType.DMA
    planes_first = jnp.transpose(chaos_field, (1, 0, 2))
    result = pl.pallas_call(
        kernel,
        out_shape=jax.ShapeDtypeStruct(planes_first.shape, F32),
        in_specs=[any_spec] * 5,
        out_specs=any_spec,
        scratch_shapes=[
            V((3, L, 1024), F32),
            V((2, 3, 1024), F32),
            V((MODES, 8), I32),
            V((POINTS, 8), I32),
            V((3 * 1024, L), F32),
            V((16, HALF + 16, L), I16),
            V((16, HALF + 16, L), I16),
            V((2, 2, 3, 1024), F32),
            V((ROWS, L), F32),
            V((ROWS, L), F32),
            V((L, L), F32),
            V((2, GROUPS, ROWS, L), F32),
            V((2 * SWEEPS, NCH, FROWS * GPC, L), BF16),
            V((2 * SWEEPS, NCH, FROWS * GPC, L), BF16),
            V((POINTS, MODES), BF16),
            V((ROWS, MODES), BF16),
            V((ROWS, POINTS), BF16),
            V((16, HALF, L), BF16),
            V((16, HALF, L), BF16),
            DMA((7,)),
            DMA((16,)),
            DMA((16,)),
            DMA((2,)),
            DMA((2,)),
            DMA((2 * SWEEPS,)),
            DMA((2 * SWEEPS, NCH)),
            DMA((16,)),
            DMA((16,)),
            DMA((3,)),
        ],
        compiler_params=pltpu.CompilerParams(
            collective_id=0, has_side_effects=True, vmem_limit_bytes=52 * 1024 * 1024
        ),
    )(planes_first, diffusivity, growth_rate, mode_table, point_index)
    return jnp.transpose(result, (1, 0, 2))


def solution(mesh):
    return jax.shard_map(
        per_device,
        mesh=mesh,
        in_specs=(P("mode", "slab", None), P("slab", None), P("slab", None), P(), P()),
        out_specs=P("mode", "slab", None),
        check_vma=False,
    )
```

```python
import functools
import jax
import jax.numpy as jnp
from jax import lax
from jax.experimental import pallas as pl
from jax.experimental.pallas import tpu as pltpu
from jax.sharding import PartitionSpec as P

MESH = pl.DeviceIdType.MESH
F32, BF16, I16, I32 = jnp.float32, jnp.bfloat16, jnp.int16, jnp.int32
MODES = 1024
POINTS = 2048
SWEEPS = 3
L = 128
GROUPS = MODES // L
ROWS = 384
HALF = ROWS // 2
NCH = 4
GPC = GROUPS // NCH
FACES = (48, 48, 48, 48, 64, 64)
OFFS = (0, 48, 96, 144, 192, 256)
FROWS = 320
COMBOS = 96
STEP = 32000.0
INV_LN2 = 1.4426950408889634


def kernel(
    x_hbm, dif_hbm, gro_hbm, mt_hbm, pi_hbm, out_hbm,
    xs, kg_src, mt, pi, hot, digit, tab, gain, snd, rcv, kg_rcv, kap, gro, cellmap,
    fld0, fld1, edge, nothing, fsnd, frcv, basis, low, react, fin, fin_rcv, done_low,
    in_sem, a_send, a_recv, kg_send, kg_recv, h_send, h_recv, f_send, f_recv, out_sem,
):
    m, s = lax.axis_index("mode"), lax.axis_index("slab")
    depth = lax.axis_size("slab") // 4
    cx, ylo = m % 4, m // 4
    core, yhi, cz = s % 2, (s // 2) % 2, s // 4
    cy = yhi * 2 + ylo

    def at(x, y, z, c):
        return ((y % 2) * 4 + x, z * 4 + (y // 2) * 2 + c)

    loads = [pltpu.make_async_copy(x_hbm.at[p], xs.at[p], in_sem.at[p]) for p in range(3)]
    loads.append(pltpu.make_async_copy(dif_hbm, kg_src.at[0], in_sem.at[3]))
    loads.append(pltpu.make_async_copy(gro_hbm, kg_src.at[1], in_sem.at[4]))
    loads.append(pltpu.make_async_copy(mt_hbm, mt, in_sem.at[5]))
    loads.append(pltpu.make_async_copy(pi_hbm, pi, in_sem.at[6]))
    for c in loads:
        c.start()

    first_plane = jnp.logical_and(cz == 0, core == 0)
    last_plane = jnp.logical_and(cz == depth - 1, core == 1)
    up = at(cx, cy, jnp.minimum(cz + core, depth - 1), 1 - core)
    down = at(cx, cy, jnp.maximum(cz + core - 1, 0), 1 - core)
    partners = (
        at((cx + 1) % 4, cy, cz, core),
        at((cx + 3) % 4, cy, cz, core),
        at(cx, (cy + 1) % 4, cz, core),
        at(cx, (cy + 3) % 4, cz, core),
        up,
        down,
    )

    barrier = pltpu.get_barrier_semaphore()
    place = (cy * 4 + cx) * 2 + core

    def greet(k, carry):
        q = (place + k) % 32
        pl.semaphore_signal(
            barrier, inc=1, device_id=at((q // 2) % 4, q // 8, cz, q % 2), device_id_type=MESH
        )
        return carry

    lax.fori_loop(1, 32, greet, 0)

    @pl.when(jnp.logical_and(core == 1, cz < depth - 1))
    def _():
        pl.semaphore_signal(barrier, inc=1, device_id=up, device_id_type=MESH)

    @pl.when(jnp.logical_and(core == 0, cz > 0))
    def _():
        pl.semaphore_signal(barrier, inc=1, device_id=down, device_id_type=MESH)

    nothing[...] = jnp.zeros_like(nothing)

    for p in range(3):
        loads[p].wait()
    big = jnp.zeros((L, L), F32)
    for p in range(3):
        for b in range(8):
            big = jnp.maximum(big, jnp.abs(xs[p, :, b * L : (b + 1) * L]))
    top = jnp.broadcast_to(jnp.max(big, axis=1, keepdims=True), (L, L))
    level = jnp.ceil(jnp.log(jnp.maximum(top, 1e-30)) * INV_LN2)
    gain[...] = jnp.exp2(-level) * STEP
    tag = jnp.transpose(level)[0:16].astype(I32).astype(I16)
    for d in range(16):
        snd[d, HALF : HALF + 16, :] = tag

    pl.semaphore_wait(
        barrier, 32 - jnp.logical_or(first_plane, last_plane).astype(I32)
    )

    def spread(j, i):
        px, py = (cx + j) % 4, (cy + i) % 4
        return pltpu.make_async_remote_copy(
            src_ref=snd.at[py * 4 + px],
            dst_ref=rcv.at[m * 2 + core],
            send_sem=a_send.at[j * 4 + i],
            recv_sem=a_recv.at[m * 2 + core],
            device_id=at(px, py, cz, yhi),
            device_id_type=MESH,
        )

    own = pltpu.make_async_copy(snd.at[cy * 4 + cx], rcv.at[m * 2 + core], a_recv.at[m * 2 + core])

    def spread_column(j, carry):
        px = (cx + j) % 4
        for p in range(3):
            for b in range(2):
                cols = pl.ds(pl.multiple_of(px * 256 + b * L, L), L)
                block = jnp.transpose(jnp.round(xs[p, :, cols] * gain[...]))
                for y in range(4):
                    tile = jnp.concatenate(
                        [block[xi * 32 + y * 8 : xi * 32 + y * 8 + 8] for xi in range(4)], axis=0
                    )
                    row = p * 64 + b * 32
                    snd[y * 4 + px, row : row + 32, :] = tile.astype(I32).astype(I16)
        for i in range(4):
            if i:
                spread(j, i).start()
            else:
                stay = jnp.logical_and(j == 0, core == yhi)

                @pl.when(stay)
                def _():
                    own.start()

                @pl.when(jnp.logical_not(stay))
                def _():
                    spread(j, 0).start()

        return carry

    lax.fori_loop(0, 4, spread_column, 0)

    loads[3].wait()
    loads[4].wait()

    def coeff(h):
        return pltpu.make_async_remote_copy(
            src_ref=kg_src,
            dst_ref=kg_rcv.at[core],
            send_sem=kg_send.at[h],
            recv_sem=kg_recv.at[core],
            device_id=(m, cz * 4 + h * 2 + yhi),
            device_id_type=MESH,
        )

    kg_own = pltpu.make_async_copy(kg_src, kg_rcv.at[core], kg_recv.at[core])

    @pl.when(core == yhi)
    def _():
        kg_own.start()
        coeff(1 - yhi).start()

    @pl.when(core != yhi)
    def _():
        coeff(yhi).start()
        coeff(1 - yhi).start()

    loads[5].wait()
    loads[6].wait()
    k8 = lax.broadcasted_iota(I32, (8, L), 0)
    power = jnp.where(
        k8 % 4 == 0, 1.0, jnp.where(k8 % 4 == 1, 3.0, jnp.where(k8 % 4 == 2, 9.0, 27.0))
    )
    degrees = mt[...].astype(F32).astype(BF16)
    pick_lane = lax.broadcasted_iota(I32, (MODES, L), 1)
    for j in range(2):
        weight = jnp.where(k8 // 4 == j, power, 0.0).astype(BF16)
        code_j = lax.dot_general(
            degrees, weight, (((0,), (0,)), ((), ())), preferred_element_type=F32
        ).astype(I32)
        for h in range(2):
            lane = pick_lane + h * L
            key = jnp.where(lane >= COMBOS, lane - COMBOS, lane)
            hot[j, :, h * L : (h + 1) * L] = jnp.where(key == code_j, 1.0, 0.0).astype(BF16)
    combo = lax.broadcasted_iota(I32, (COMBOS, 256), 0)
    for d in range(4):
        digit[d] = (combo // 3**d) % 3
        tab[:, 2 * COMBOS : 256, :] = jnp.zeros((2, 256 - 2 * COMBOS, 256), BF16)
    QB = 256

    def build(i, carry):
        cols = pl.ds(pl.multiple_of(i * QB, QB), QB)
        first = (pi[:, cols].astype(F32) - 3.0) * 0.32
        second = (first * first - 1.0) * 0.7071067811865476
        picked = []
        for j in range(2):
            for t in range(COMBOS // 16):
                halves = []
                for u in range(2):
                    r = t * 16 + u * 8
                    result = None
                    for d in range(4):
                        h1 = jnp.broadcast_to(first[j * 4 + d : j * 4 + d + 1], (8, QB))
                        h2 = jnp.broadcast_to(second[j * 4 + d : j * 4 + d + 1], (8, QB))
                        which = digit[d, r : r + 8, :]
                        factor = jnp.where(which == 0, 1.0, jnp.where(which == 1, h1, h2))
                        result = factor if result is None else result * factor
                    halves.append(result)
                both = jnp.concatenate(halves, axis=0)
                high = both.astype(BF16)
                tab[j, t * 16 : t * 16 + 16, :] = high
                tab[j, COMBOS + t * 16 : COMBOS + t * 16 + 16, :] = (
                    both - high.astype(F32)
                ).astype(BF16)
        for half in range(MODES // 256):
            rows = slice(half * 256, half * 256 + 256)
            picked = [
                jnp.dot(hot[j, rows, :], tab[j], preferred_element_type=F32) for j in range(2)
            ]
            basis[rows, cols] = (picked[0] * picked[1]).astype(BF16)
        return carry

    lax.fori_loop(0, POINTS // QB, build, 0)

    for c in range(2):
        pltpu.make_async_copy(kg_rcv.at[c], kg_rcv.at[c], kg_recv.at[c]).wait()
    for c in range(2):
        for b in range(2):
            cols = pl.ds(pl.multiple_of(cx * 256 + b * L, L), L)
            rows8 = [kg_rcv[c, 0, :, cols], kg_rcv[c, 1, :, cols], jnp.zeros((L - 6, L), F32)]
            cellmap[...] = jnp.transpose(jnp.concatenate(rows8, axis=0))
            for xi in range(4):
                tile = cellmap[pl.ds(pl.multiple_of(xi * 32 + cy * 8, 8), 8), :]
                for p in range(3):
                    to = (c * 3 + p) * 64 + (b * 4 + xi) * 8
                    kap[to : to + 8, :] = jnp.broadcast_to(tile[:, p : p + 1], (8, L))
                    gro[to : to + 8, :] = jnp.broadcast_to(tile[:, 3 + p : 4 + p], (8, L)) * 0.125

    def face_copy(sw, ch, f):
        rows = pl.ds(OFFS[f] * GPC, FACES[f] * GPC)
        return pltpu.make_async_remote_copy(
            src_ref=fsnd.at[sw, ch, rows],
            dst_ref=frcv.at[sw, ch, rows],
            send_sem=h_send.at[sw, max(f - 3, 0)],
            recv_sem=h_recv.at[sw, ch],
            device_id=partners[f],
            device_id_type=MESH,
        )

    def end_copy(sw, ch, f):
        rows = pl.ds(OFFS[f] * GPC, FACES[f] * GPC)
        return pltpu.make_async_copy(nothing, frcv.at[sw, ch, rows], h_recv.at[sw, ch])

    def send_faces(sw, fld, ch):
        for gg in range(GPC):
            g = ch * GPC + gg

            def put(f, value):
                row = OFFS[f] * GPC + gg * FACES[f]
                fsnd[sw, ch, row : row + FACES[f], :] = value.astype(BF16)

            put(0, jnp.concatenate([fld[g, z * 64 + 56 : z * 64 + 64, :] for z in range(6)], 0))
            put(1, jnp.concatenate([fld[g, z * 64 : z * 64 + 8, :] for z in range(6)], 0))
            put(2, jnp.concatenate([fld[g, pl.ds(z * 64 + 7, 8, stride=8), :] for z in range(6)], 0))
            put(3, jnp.concatenate([fld[g, pl.ds(z * 64, 8, stride=8), :] for z in range(6)], 0))
            put(4, fld[g, 320:384, :])
            put(5, fld[g, 0:64, :])

        for f in range(4):
            face_copy(sw, ch, f).start()

        @pl.when(jnp.logical_not(last_plane))
        def _():
            face_copy(sw, ch, 4).start()

        @pl.when(last_plane)
        def _():
            end_copy(sw, ch, 5).start()

        @pl.when(jnp.logical_not(first_plane))
        def _():
            face_copy(sw, ch, 5).start()

        @pl.when(first_plane)
        def _():
            end_copy(sw, ch, 4).start()

    sub = lax.broadcasted_iota(I32, (8, L), 0)

    def sweep(sw, old, new, ch):
        pltpu.make_async_copy(frcv.at[sw, ch], frcv.at[sw, ch], h_recv.at[sw, ch]).wait()
        for gg in range(GPC):
            g = ch * GPC + gg

            def halo(f):
                row = OFFS[f] * GPC + gg * FACES[f]
                return frcv[sw, ch, row : row + FACES[f], :].astype(F32)

            xl, xh, yl, yh, zl, zh = [halo(f) for f in range(6)]
            for z in range(6):
                edge[gg, pl.ds(z * 64, 8, stride=8), :] = yl[z * 8 : z * 8 + 8]
                edge[gg, pl.ds(z * 64 + 7, 8, stride=8), :] = yh[z * 8 : z * 8 + 8]
            for z in range(6):
                for x in range(8):
                    r = z * 64 + x * 8
                    mid = old[g, r : r + 8, :]
                    xm = old[g, r - 8 : r, :] if x else xl[z * 8 : z * 8 + 8]
                    xp = old[g, r + 8 : r + 16, :] if x < 7 else xh[z * 8 : z * 8 + 8]
                    zm = old[g, r - 64 : r - 56, :] if z else zl[x * 8 : x * 8 + 8]
                    zp = old[g, r + 64 : r + 72, :] if z < 5 else zh[x * 8 : x * 8 + 8]
                    ends = edge[gg, r : r + 8, :]
                    ym = jnp.where(sub == 0, ends, pltpu.roll(mid, 1, 0))
                    yp = jnp.where(sub == 7, ends, pltpu.roll(mid, 7, 0))
                    total = ((xm + xp) + (ym + yp)) + (zp + zm)
                    new[g, r : r + 8, :] = mid + kap[r : r + 8, :] * (total - 6.0 * mid)

    def lower(fld, ch):
        for gg in range(GPC):
            col = pl.ds(pl.multiple_of((ch * GPC + gg) * L, L), L)
            low[:, col] = fld[ch * GPC + gg].astype(BF16)

    def diffuse(first_sweep, here, there):
        for t in range(SWEEPS):
            sw = first_sweep + t

            def one(ch, carry, t=t, sw=sw, here=here, there=there):
                sweep(sw, here, there, ch)
                if t < SWEEPS - 1:
                    send_faces(sw + 1, there, ch)
                else:
                    lower(there, ch)
                return carry

            lax.fori_loop(0, NCH, one, 0)
            here, there = there, here

    QC = 256

    def forward():
        for i in range(POINTS // QC):
            at_q = slice(i * QC, (i + 1) * QC)
            v = jnp.dot(low[...], basis[:, at_q], preferred_element_type=F32)
            rate = jnp.concatenate([gro[...]] * (QC // L), axis=1)
            react[:, at_q] = (v * (rate - (v * v) * (1.0 / 128.0))).astype(BF16)

    def increment(ch):
        cols = slice(ch * GPC * L, (ch + 1) * GPC * L)
        inc = lax.dot_general(
            react[...], basis[cols, :], (((1,), (1,)), ((), ())), preferred_element_type=F32
        )
        return inc * (1.4 * MODES**0.5 / POINTS)

    def arrive(ch, carry):
        def one(gg, carry):
            g = ch * GPC + gg
            for c in range(2):
                slot = g * 2 + c
                pltpu.make_async_copy(rcv.at[slot], rcv.at[slot], a_recv.at[slot]).wait()
                level = rcv[slot, HALF : HALF + 16, :].astype(I32).astype(F32)[0:1]
                unit = jnp.exp2(level) * (1.0 / STEP)
                fld0[g, c * HALF : (c + 1) * HALF, :] = (
                    rcv[slot, 0:HALF, :].astype(I32).astype(F32) * unit
                )
            return carry

        lax.fori_loop(0, GPC, one, 0)
        send_faces(0, fld0, ch)
        return carry

    lax.fori_loop(0, NCH, arrive, 0)

    diffuse(0, fld0, fld1)
    forward()
    for ch in range(NCH):
        inc = increment(ch)
        for gg in range(GPC):
            fld1[ch * GPC + gg] += inc[:, gg * L : (gg + 1) * L]
        send_faces(SWEEPS, fld1, ch)
    diffuse(SWEEPS, fld1, fld0)
    forward()

    patch = cy * 4 + cx

    def home(g, c):
        return pltpu.make_async_remote_copy(
            src_ref=fin.at[g * 2 + c],
            dst_ref=fin_rcv.at[patch],
            send_sem=f_send.at[g * 2 + c],
            recv_sem=f_recv.at[patch],
            device_id=(g, cz * 4 + core * 2 + c),
            device_id_type=MESH,
        )

    def stays(g, c):
        return pltpu.make_async_copy(fin.at[g * 2 + c], fin_rcv.at[patch], f_recv.at[patch])

    def is_own(g, c):
        return jnp.logical_and(g == m, jnp.logical_and(core == yhi, c == core))

    for ch in range(NCH):
        inc = increment(ch)
        for gg in range(GPC):
            g = ch * GPC + gg
            done = (fld0[g] + inc[:, gg * L : (gg + 1) * L]).astype(BF16)
            for c in range(2):
                fin[g * 2 + c] = done[c * HALF : (c + 1) * HALF]

                @pl.when(is_own(g, c))
                def _():
                    stays(g, c).start()

                @pl.when(jnp.logical_not(is_own(g, c)))
                def _():
                    home(g, c).start()


    def out_copy(px):
        cols = pl.ds(pl.multiple_of(px * 256, 256), 256)
        return pltpu.make_async_copy(
            done_low.at[:, :, cols], out_hbm.at[:, :, cols], out_sem.at[px]
        )

    def collect(j, carry):
        px = (cx + j + (j // 2) * (5 - 2 * j)) % 4
        for y in range(4):
            slot = y * 4 + px
            pltpu.make_async_copy(fin_rcv.at[slot], fin_rcv.at[slot], f_recv.at[slot]).wait()
        for p in range(3):
            for b in range(2):
                row = p * 64 + b * 32
                parts = [fin_rcv[y * 4 + px, row : row + 32, :].astype(F32) for y in range(4)]
                block = jnp.concatenate(
                    [parts[y][xi * 8 : xi * 8 + 8] for xi in range(4) for y in range(4)], axis=0
                )
                cols = pl.ds(pl.multiple_of(px * 256 + b * L, L), L)
                done_low[p, :, cols] = jnp.transpose(block).astype(BF16)
        out_copy(px).start()
        return carry

    lax.fori_loop(0, 4, collect, 0)

    @pl.when(core != yhi)
    def _():
        spread(0, 0).wait_send()
        coeff(yhi).wait_send()
        coeff(1 - yhi).wait_send()

    @pl.when(core == yhi)
    def _():
        coeff(1 - yhi).wait_send()

    def spread_done(k, carry):
        spread(k // 4, k % 4).wait_send()
        return carry

    lax.fori_loop(1, 16, spread_done, 0)

    def faces_done(sw, carry):
        def sent(f, lo, hi):
            part = fsnd.at[sw, :, pl.ds(lo * GPC, (hi - lo) * GPC)]
            pltpu.make_async_copy(part, part, h_send.at[sw, f]).wait()

        sent(0, 0, 192)

        @pl.when(jnp.logical_not(last_plane))
        def _():
            sent(1, 192, 256)

        @pl.when(jnp.logical_not(first_plane))
        def _():
            sent(2, 256, 320)

        return carry

    lax.fori_loop(0, 2 * SWEEPS, faces_done, 0)

    def home_done(i, carry):
        g, c = i // 2, i % 2

        @pl.when(jnp.logical_not(is_own(g, c)))
        def _():
            home(g, c).wait_send()

        return carry

    lax.fori_loop(0, 16, home_done, 0)
    for px in range(4):
        out_copy(px).wait()


def per_device(chaos_field, diffusivity, growth_rate, mode_table, point_index):
    any_spec = pl.BlockSpec(memory_space=pl.ANY)
    V = pltpu.VMEM
    DMA = pltpu.SemaphoreType.DMA
    planes_first = jnp.transpose(chaos_field, (1, 0, 2))
    result = pl.pallas_call(
        kernel,
        out_shape=jax.ShapeDtypeStruct(planes_first.shape, BF16),
        in_specs=[pl.BlockSpec(memory_space=pltpu.HBM)] * 5,
        out_specs=any_spec,
        scratch_shapes=[
            V((3, L, 1024), F32),
            V((2, 3, 1024), F32),
            V((8, MODES), I32),
            V((8, POINTS), I32),
            V((2, MODES, 256), BF16),
            V((4, COMBOS, 256), I32),
            V((2, 256, 256), BF16),
            V((L, L), F32),
            V((16, HALF + 16, L), I16),
            V((16, HALF + 16, L), I16),
            V((2, 2, 3, 1024), F32),
            V((ROWS, L), F32),
            V((ROWS, L), F32),
            V((L, L), F32),
            V((GROUPS, ROWS, L), F32),
            V((GROUPS, ROWS, L), F32),
            V((GPC, ROWS, L), F32),
            V((64 * GPC, L), BF16),
            V((2 * SWEEPS, NCH, FROWS * GPC, L), BF16),
            V((2 * SWEEPS, NCH, FROWS * GPC, L), BF16),
            V((MODES, POINTS), BF16),
            V((ROWS, MODES), BF16),
            V((ROWS, POINTS), BF16),
            V((16, HALF, L), BF16),
            V((16, HALF, L), BF16),
            V((3, L, 1024), BF16),
            DMA((7,)),
            DMA((16,)),
            DMA((16,)),
            DMA((2,)),
            DMA((2,)),
            DMA((2 * SWEEPS, 3)),
            DMA((2 * SWEEPS, NCH)),
            DMA((16,)),
            DMA((16,)),
            DMA((4,)),
        ],
        compiler_params=pltpu.CompilerParams(
            collective_id=0, has_side_effects=True, vmem_limit_bytes=52 * 1024 * 1024
        ),
    )(planes_first, diffusivity, growth_rate, mode_table.T, point_index.T)
    return jnp.transpose(result.astype(F32), (1, 0, 2))


def solution(mesh):
    return jax.shard_map(
        per_device,
        mesh=mesh,
        in_specs=(P("mode", "slab", None), P("slab", None), P("slab", None), P(), P()),
        out_specs=P("mode", "slab", None),
        check_vma=False,
    )
```

```python
import functools
import jax
import jax.numpy as jnp
from jax import lax
from jax.experimental import pallas as pl
from jax.experimental.pallas import tpu as pltpu
from jax.sharding import PartitionSpec as P

MESH = pl.DeviceIdType.MESH
F32, BF16, I16, I32 = jnp.float32, jnp.bfloat16, jnp.int16, jnp.int32
MODES = 1024
POINTS = 2048
SWEEPS = 3
L = 128
GROUPS = MODES // L
ROWS = 384
HALF = ROWS // 2
NCH = 4
GPC = GROUPS // NCH
FACES = (48, 48, 48, 48, 64, 64)
OFFS = (0, 48, 96, 144, 192, 256)
FROWS = 320
FAR = (2, 1, 3, 0)
COMBOS = 96
STEP = 32000.0
INV_LN2 = 1.4426950408889634


def kernel(
    x_hbm, dif_hbm, gro_hbm, mt_hbm, pi_hbm, out_hbm,
    xs, kg_src, mt, pi, hot, digit, tab, gain, snd, rcv, kg_rcv, kap, gro, cellmap,
    fld0, fld1, edge, nothing, fsnd, frcv, basis, values, react, fin, fin_rcv, done_low,
    in_sem, a_send, a_recv, kg_send, kg_recv, h_send, h_recv, f_send, f_recv, out_sem,
):
    m, s = lax.axis_index("mode"), lax.axis_index("slab")
    depth = lax.axis_size("slab") // 4
    cx, ylo = m % 4, m // 4
    core, yhi, cz = s % 2, (s // 2) % 2, s // 4
    cy = yhi * 2 + ylo

    def at(x, y, z, c):
        return ((y % 2) * 4 + x, z * 4 + (y // 2) * 2 + c)

    loads = [pltpu.make_async_copy(x_hbm.at[p], xs.at[p], in_sem.at[p]) for p in range(3)]
    loads.append(pltpu.make_async_copy(dif_hbm, kg_src.at[0], in_sem.at[3]))
    loads.append(pltpu.make_async_copy(gro_hbm, kg_src.at[1], in_sem.at[4]))
    loads.append(pltpu.make_async_copy(mt_hbm, mt, in_sem.at[5]))
    loads.append(pltpu.make_async_copy(pi_hbm, pi, in_sem.at[6]))
    for c in loads:
        c.start()

    first_plane = jnp.logical_and(cz == 0, core == 0)
    last_plane = jnp.logical_and(cz == depth - 1, core == 1)
    up = at(cx, cy, jnp.minimum(cz + core, depth - 1), 1 - core)
    down = at(cx, cy, jnp.maximum(cz + core - 1, 0), 1 - core)
    partners = (
        at((cx + 1) % 4, cy, cz, core),
        at((cx + 3) % 4, cy, cz, core),
        at(cx, (cy + 1) % 4, cz, core),
        at(cx, (cy + 3) % 4, cz, core),
        up,
        down,
    )

    barrier = pltpu.get_barrier_semaphore()
    place = (cy * 4 + cx) * 2 + core

    def greet(k, carry):
        q = (place + k) % 32
        pl.semaphore_signal(
            barrier, inc=1, device_id=at((q // 2) % 4, q // 8, cz, q % 2), device_id_type=MESH
        )
        return carry

    lax.fori_loop(1, 32, greet, 0)

    @pl.when(jnp.logical_and(core == 1, cz < depth - 1))
    def _():
        pl.semaphore_signal(barrier, inc=1, device_id=up, device_id_type=MESH)

    @pl.when(jnp.logical_and(core == 0, cz > 0))
    def _():
        pl.semaphore_signal(barrier, inc=1, device_id=down, device_id_type=MESH)

    nothing[...] = jnp.zeros_like(nothing)

    for p in range(3):
        loads[p].wait()
    big = jnp.zeros((L, L), F32)
    for p in range(3):
        for b in range(8):
            big = jnp.maximum(big, jnp.abs(xs[p, :, b * L : (b + 1) * L]))
    top = jnp.broadcast_to(jnp.max(big, axis=1, keepdims=True), (L, L))
    level = jnp.ceil(jnp.log(jnp.maximum(top, 1e-30)) * INV_LN2)
    gain[...] = jnp.exp2(-level) * STEP
    tag = jnp.transpose(level)[0:16].astype(I32).astype(I16)
    for d in range(16):
        snd[d, HALF : HALF + 16, :] = tag

    def spread(j, i):
        px, py = (cx + j) % 4, (cy + i) % 4
        return pltpu.make_async_remote_copy(
            src_ref=snd.at[py * 4 + px],
            dst_ref=rcv.at[m * 2 + core],
            send_sem=a_send.at[j * 4 + i],
            recv_sem=a_recv.at[m * 2 + core],
            device_id=at(px, py, cz, yhi),
            device_id_type=MESH,
        )

    own = pltpu.make_async_copy(snd.at[cy * 4 + cx], rcv.at[m * 2 + core], a_recv.at[m * 2 + core])

    def code_column(n):
        px = (cx + FAR[n]) % 4
        for p in range(3):
            for b in range(2):
                cols = pl.ds(pl.multiple_of(px * 256 + b * L, L), L)
                block = jnp.transpose(jnp.round(xs[p, :, cols] * gain[...]))
                for y in range(4):
                    tile = jnp.concatenate(
                        [block[xi * 32 + y * 8 : xi * 32 + y * 8 + 8] for xi in range(4)], axis=0
                    )
                    row = p * 64 + b * 32
                    snd[y * 4 + px, row : row + 32, :] = tile.astype(I32).astype(I16)

    def spread_column(n):
        j = FAR[n]
        for i in FAR:
            if i or j:
                spread(j, i).start()
            else:

                @pl.when(core == yhi)
                def _():
                    own.start()

                @pl.when(core != yhi)
                def _():
                    spread(0, 0).start()

    code_column(0)
    pl.semaphore_wait(
        barrier, 32 - jnp.logical_or(first_plane, last_plane).astype(I32)
    )
    spread_column(0)
    for n in range(1, 4):
        code_column(n)
        spread_column(n)

    loads[3].wait()
    loads[4].wait()

    def coeff(h):
        return pltpu.make_async_remote_copy(
            src_ref=kg_src,
            dst_ref=kg_rcv.at[core],
            send_sem=kg_send.at[h],
            recv_sem=kg_recv.at[core],
            device_id=(m, cz * 4 + h * 2 + yhi),
            device_id_type=MESH,
        )

    kg_own = pltpu.make_async_copy(kg_src, kg_rcv.at[core], kg_recv.at[core])

    @pl.when(core == yhi)
    def _():
        kg_own.start()
        coeff(1 - yhi).start()

    @pl.when(core != yhi)
    def _():
        coeff(yhi).start()
        coeff(1 - yhi).start()

    loads[5].wait()
    loads[6].wait()
    k8 = lax.broadcasted_iota(I32, (8, L), 0)
    power = jnp.where(
        k8 % 4 == 0, 1.0, jnp.where(k8 % 4 == 1, 3.0, jnp.where(k8 % 4 == 2, 9.0, 27.0))
    )
    degrees = mt[...].astype(F32).astype(BF16)
    pick_lane = lax.broadcasted_iota(I32, (MODES, L), 1)
    for j in range(2):
        weight = jnp.where(k8 // 4 == j, power, 0.0).astype(BF16)
        code_j = lax.dot_general(
            degrees, weight, (((0,), (0,)), ((), ())), preferred_element_type=F32
        ).astype(I32)
        for h in range(2):
            lane = pick_lane + h * L
            key = jnp.where(lane >= COMBOS, lane - COMBOS, lane)
            hot[j, :, h * L : (h + 1) * L] = jnp.where(key == code_j, 1.0, 0.0).astype(BF16)
    combo = lax.broadcasted_iota(I32, (COMBOS, 256), 0)
    for d in range(4):
        digit[d] = (combo // 3**d) % 3
        tab[:, 2 * COMBOS : 256, :] = jnp.zeros((2, 256 - 2 * COMBOS, 256), BF16)
    QB = 256

    def build(i, carry):
        cols = pl.ds(pl.multiple_of(i * QB, QB), QB)
        first = (pi[:, cols].astype(F32) - 3.0) * 0.32
        second = (first * first - 1.0) * 0.7071067811865476
        picked = []
        for j in range(2):
            for t in range(COMBOS // 16):
                halves = []
                for u in range(2):
                    r = t * 16 + u * 8
                    result = None
                    for d in range(4):
                        h1 = jnp.broadcast_to(first[j * 4 + d : j * 4 + d + 1], (8, QB))
                        h2 = jnp.broadcast_to(second[j * 4 + d : j * 4 + d + 1], (8, QB))
                        which = digit[d, r : r + 8, :]
                        factor = jnp.where(which == 0, 1.0, jnp.where(which == 1, h1, h2))
                        result = factor if result is None else result * factor
                    halves.append(result)
                both = jnp.concatenate(halves, axis=0)
                high = both.astype(BF16)
                tab[j, t * 16 : t * 16 + 16, :] = high
                tab[j, COMBOS + t * 16 : COMBOS + t * 16 + 16, :] = (
                    both - high.astype(F32)
                ).astype(BF16)
        for half in range(MODES // 256):
            rows = slice(half * 256, half * 256 + 256)
            picked = [
                jnp.dot(hot[j, rows, :], tab[j], preferred_element_type=F32) for j in range(2)
            ]
            basis[rows, cols] = (picked[0] * picked[1]).astype(BF16)
        return carry

    lax.fori_loop(0, POINTS // QB, build, 0)

    for c in range(2):
        pltpu.make_async_copy(kg_rcv.at[c], kg_rcv.at[c], kg_recv.at[c]).wait()
    for c in range(2):
        for b in range(2):
            cols = pl.ds(pl.multiple_of(cx * 256 + b * L, L), L)
            rows8 = [kg_rcv[c, 0, :, cols], kg_rcv[c, 1, :, cols], jnp.zeros((L - 6, L), F32)]
            cellmap[...] = jnp.transpose(jnp.concatenate(rows8, axis=0))
            for xi in range(4):
                tile = cellmap[pl.ds(pl.multiple_of(xi * 32 + cy * 8, 8), 8), :]
                for p in range(3):
                    to = (c * 3 + p) * 64 + (b * 4 + xi) * 8
                    kap[to : to + 8, :] = jnp.broadcast_to(tile[:, p : p + 1], (8, L))
                    gro[to : to + 8, :] = jnp.broadcast_to(tile[:, 3 + p : 4 + p], (8, L)) * 0.125

    def face_copy(sw, ch, f):
        rows = pl.ds(OFFS[f] * GPC, FACES[f] * GPC)
        return pltpu.make_async_remote_copy(
            src_ref=fsnd.at[sw, ch, rows],
            dst_ref=frcv.at[sw, ch, rows],
            send_sem=h_send.at[sw, max(f - 3, 0)],
            recv_sem=h_recv.at[sw, ch],
            device_id=partners[f],
            device_id_type=MESH,
        )

    def end_copy(sw, ch, f):
        rows = pl.ds(OFFS[f] * GPC, FACES[f] * GPC)
        return pltpu.make_async_copy(nothing, frcv.at[sw, ch, rows], h_recv.at[sw, ch])

    def send_faces(sw, fld, ch):
        for gg in range(GPC):
            g = ch * GPC + gg

            def put(f, value):
                row = OFFS[f] * GPC + gg * FACES[f]
                fsnd[sw, ch, row : row + FACES[f], :] = value.astype(BF16)

            put(0, jnp.concatenate([fld[g, z * 64 + 56 : z * 64 + 64, :] for z in range(6)], 0))
            put(1, jnp.concatenate([fld[g, z * 64 : z * 64 + 8, :] for z in range(6)], 0))
            put(2, jnp.concatenate([fld[g, pl.ds(z * 64 + 7, 8, stride=8), :] for z in range(6)], 0))
            put(3, jnp.concatenate([fld[g, pl.ds(z * 64, 8, stride=8), :] for z in range(6)], 0))
            put(4, fld[g, 320:384, :])
            put(5, fld[g, 0:64, :])

        for f in range(4):
            face_copy(sw, ch, f).start()

        @pl.when(jnp.logical_not(last_plane))
        def _():
            face_copy(sw, ch, 4).start()

        @pl.when(last_plane)
        def _():
            end_copy(sw, ch, 5).start()

        @pl.when(jnp.logical_not(first_plane))
        def _():
            face_copy(sw, ch, 5).start()

        @pl.when(first_plane)
        def _():
            end_copy(sw, ch, 4).start()

    sub = lax.broadcasted_iota(I32, (8, L), 0)

    def sweep(sw, old, new, ch):
        pltpu.make_async_copy(frcv.at[sw, ch], frcv.at[sw, ch], h_recv.at[sw, ch]).wait()
        for gg in range(GPC):
            g = ch * GPC + gg

            def halo(f):
                row = OFFS[f] * GPC + gg * FACES[f]
                return frcv[sw, ch, row : row + FACES[f], :].astype(F32)

            xl, xh, yl, yh, zl, zh = [halo(f) for f in range(6)]
            for z in range(6):
                edge[gg, pl.ds(z * 64, 8, stride=8), :] = yl[z * 8 : z * 8 + 8]
                edge[gg, pl.ds(z * 64 + 7, 8, stride=8), :] = yh[z * 8 : z * 8 + 8]
            for z in range(6):
                for x in range(8):
                    r = z * 64 + x * 8
                    mid = old[g, r : r + 8, :]
                    xm = old[g, r - 8 : r, :] if x else xl[z * 8 : z * 8 + 8]
                    xp = old[g, r + 8 : r + 16, :] if x < 7 else xh[z * 8 : z * 8 + 8]
                    zm = old[g, r - 64 : r - 56, :] if z else zl[x * 8 : x * 8 + 8]
                    zp = old[g, r + 64 : r + 72, :] if z < 5 else zh[x * 8 : x * 8 + 8]
                    ends = edge[gg, r : r + 8, :]
                    ym = jnp.where(sub == 0, ends, pltpu.roll(mid, 1, 0))
                    yp = jnp.where(sub == 7, ends, pltpu.roll(mid, 7, 0))
                    total = ((xm + xp) + (ym + yp)) + (zp + zm)
                    new[g, r : r + 8, :] = mid + kap[r : r + 8, :] * (total - 6.0 * mid)

    QC = 256

    def forward(fld, ch):
        part = jnp.concatenate([fld[ch * GPC + gg].astype(BF16) for gg in range(GPC)], axis=1)
        rows = slice(ch * GPC * L, (ch + 1) * GPC * L)
        for i in range(POINTS // QC):
            at_q = slice(i * QC, (i + 1) * QC)
            v = jnp.dot(part, basis[rows, at_q], preferred_element_type=F32)
            if ch:
                v = values[:, at_q] + v
            if ch < NCH - 1:
                values[:, at_q] = v
            else:
                rate = jnp.concatenate([gro[...]] * (QC // L), axis=1)
                react[:, at_q] = (v * (rate - (v * v) * (1.0 / 128.0))).astype(BF16)

    def diffuse(first_sweep, here, there):
        for t in range(SWEEPS - 1):
            sw = first_sweep + t

            def one(ch, carry, sw=sw, here=here, there=there):
                sweep(sw, here, there, ch)
                send_faces(sw + 1, there, ch)
                return carry

            lax.fori_loop(0, NCH, one, 0)
            here, there = there, here
        for ch in range(NCH):
            sweep(first_sweep + SWEEPS - 1, here, there, ch)
            forward(there, ch)

    def increment(ch):
        cols = slice(ch * GPC * L, (ch + 1) * GPC * L)
        inc = lax.dot_general(
            react[...], basis[cols, :], (((1,), (1,)), ((), ())), preferred_element_type=F32
        )
        return inc * (1.4 * MODES**0.5 / POINTS)

    def arrive(ch, carry):
        def one(gg, carry):
            g = ch * GPC + gg
            for c in range(2):
                slot = g * 2 + c
                pltpu.make_async_copy(rcv.at[slot], rcv.at[slot], a_recv.at[slot]).wait()
                level = rcv[slot, HALF : HALF + 16, :].astype(I32).astype(F32)[0:1]
                unit = jnp.exp2(level) * (1.0 / STEP)
                fld0[g, c * HALF : (c + 1) * HALF, :] = (
                    rcv[slot, 0:HALF, :].astype(I32).astype(F32) * unit
                )
            return carry

        lax.fori_loop(0, GPC, one, 0)
        send_faces(0, fld0, ch)
        return carry

    lax.fori_loop(0, NCH, arrive, 0)

    diffuse(0, fld0, fld1)
    for ch in range(NCH):
        inc = increment(ch)
        for gg in range(GPC):
            fld1[ch * GPC + gg] += inc[:, gg * L : (gg + 1) * L]
        send_faces(SWEEPS, fld1, ch)
    diffuse(SWEEPS, fld1, fld0)

    patch = cy * 4 + cx

    def home(g, c):
        return pltpu.make_async_remote_copy(
            src_ref=fin.at[g * 2 + c],
            dst_ref=fin_rcv.at[patch],
            send_sem=f_send.at[g * 2 + c],
            recv_sem=f_recv.at[patch],
            device_id=(g, cz * 4 + core * 2 + c),
            device_id_type=MESH,
        )

    def stays(g, c):
        return pltpu.make_async_copy(fin.at[g * 2 + c], fin_rcv.at[patch], f_recv.at[patch])

    def is_own(g, c):
        return jnp.logical_and(g == m, jnp.logical_and(core == yhi, c == core))

    for ch in range(NCH):
        inc = increment(ch)
        for gg in range(GPC):
            g = ch * GPC + gg
            done = (fld0[g] + inc[:, gg * L : (gg + 1) * L]).astype(BF16)
            for c in range(2):
                fin[g * 2 + c] = done[c * HALF : (c + 1) * HALF]

                @pl.when(is_own(g, c))
                def _():
                    stays(g, c).start()

                @pl.when(jnp.logical_not(is_own(g, c)))
                def _():
                    home(g, c).start()


    def out_copy(px):
        cols = pl.ds(pl.multiple_of(px * 256, 256), 256)
        return pltpu.make_async_copy(
            done_low.at[:, :, cols], out_hbm.at[:, :, cols], out_sem.at[px]
        )

    def collect(j, carry):
        px = (cx + j + (j // 2) * (5 - 2 * j)) % 4
        for y in range(4):
            slot = y * 4 + px
            pltpu.make_async_copy(fin_rcv.at[slot], fin_rcv.at[slot], f_recv.at[slot]).wait()
        for p in range(3):
            for b in range(2):
                row = p * 64 + b * 32
                parts = [fin_rcv[y * 4 + px, row : row + 32, :].astype(F32) for y in range(4)]
                block = jnp.concatenate(
                    [parts[y][xi * 8 : xi * 8 + 8] for xi in range(4) for y in range(4)], axis=0
                )
                cols = pl.ds(pl.multiple_of(px * 256 + b * L, L), L)
                done_low[p, :, cols] = jnp.transpose(block).astype(BF16)
        out_copy(px).start()
        return carry

    lax.fori_loop(0, 4, collect, 0)

    @pl.when(core != yhi)
    def _():
        spread(0, 0).wait_send()
        coeff(yhi).wait_send()
        coeff(1 - yhi).wait_send()

    @pl.when(core == yhi)
    def _():
        coeff(1 - yhi).wait_send()

    def spread_done(k, carry):
        spread(k // 4, k % 4).wait_send()
        return carry

    lax.fori_loop(1, 16, spread_done, 0)

    def faces_done(sw, carry):
        def sent(f, lo, hi):
            part = fsnd.at[sw, :, pl.ds(lo * GPC, (hi - lo) * GPC)]
            pltpu.make_async_copy(part, part, h_send.at[sw, f]).wait()

        sent(0, 0, 192)

        @pl.when(jnp.logical_not(last_plane))
        def _():
            sent(1, 192, 256)

        @pl.when(jnp.logical_not(first_plane))
        def _():
            sent(2, 256, 320)

        return carry

    lax.fori_loop(0, 2 * SWEEPS, faces_done, 0)

    def home_done(i, carry):
        g, c = i // 2, i % 2

        @pl.when(jnp.logical_not(is_own(g, c)))
        def _():
            home(g, c).wait_send()

        return carry

    lax.fori_loop(0, 16, home_done, 0)
    for px in range(4):
        out_copy(px).wait()


def per_device(chaos_field, diffusivity, growth_rate, mode_table, point_index):
    any_spec = pl.BlockSpec(memory_space=pl.ANY)
    V = pltpu.VMEM
    DMA = pltpu.SemaphoreType.DMA
    planes_first = jnp.transpose(chaos_field, (1, 0, 2))
    result = pl.pallas_call(
        kernel,
        out_shape=jax.ShapeDtypeStruct(planes_first.shape, BF16),
        in_specs=[any_spec] * 5,
        out_specs=any_spec,
        scratch_shapes=[
            V((3, L, 1024), F32),
            V((2, 3, 1024), F32),
            V((8, MODES), I32),
            V((8, POINTS), I32),
            V((2, MODES, 256), BF16),
            V((4, COMBOS, 256), I32),
            V((2, 256, 256), BF16),
            V((L, L), F32),
            V((16, HALF + 16, L), I16),
            V((16, HALF + 16, L), I16),
            V((2, 2, 3, 1024), F32),
            V((ROWS, L), F32),
            V((ROWS, L), F32),
            V((L, L), F32),
            V((GROUPS, ROWS, L), F32),
            V((GROUPS, ROWS, L), F32),
            V((GPC, ROWS, L), F32),
            V((64 * GPC, L), BF16),
            V((2 * SWEEPS, NCH, FROWS * GPC, L), BF16),
            V((2 * SWEEPS, NCH, FROWS * GPC, L), BF16),
            V((MODES, POINTS), BF16),
            V((ROWS, POINTS), F32),
            V((ROWS, POINTS), BF16),
            V((16, HALF, L), BF16),
            V((16, HALF, L), BF16),
            V((3, L, 1024), BF16),
            DMA((7,)),
            DMA((16,)),
            DMA((16,)),
            DMA((2,)),
            DMA((2,)),
            DMA((2 * SWEEPS, 3)),
            DMA((2 * SWEEPS, NCH)),
            DMA((16,)),
            DMA((16,)),
            DMA((4,)),
        ],
        compiler_params=pltpu.CompilerParams(
            collective_id=0, has_side_effects=True, vmem_limit_bytes=58 * 1024 * 1024
        ),
    )(planes_first, diffusivity, growth_rate, mode_table.T, point_index.T)
    return jnp.transpose(result.astype(F32), (1, 0, 2))


def solution(mesh):
    return jax.shard_map(
        per_device,
        mesh=mesh,
        in_specs=(P("mode", "slab", None), P("slab", None), P("slab", None), P(), P()),
        out_specs=P("mode", "slab", None),
        check_vma=False,
    )
```

```python
import functools
import jax
import jax.numpy as jnp
from jax import lax
from jax.experimental import pallas as pl
from jax.experimental.pallas import tpu as pltpu
from jax.sharding import PartitionSpec as P

MESH = pl.DeviceIdType.MESH
F32, BF16, I32 = jnp.float32, jnp.bfloat16, jnp.int32
MODES = 1024
POINTS = 2048
SWEEPS = 3
L = 128
GROUPS = MODES // L
ROWS = 384
HALF = ROWS // 2
NCH = 4
GPC = GROUPS // NCH
FACES = (48, 48, 48, 48, 64, 64)
OFFS = (0, 48, 96, 144, 192, 256)
FROWS = 320
FAR = (2, 1, 3, 0)
COMBOS = 96


def kernel(
    x_hbm, dif_hbm, gro_hbm, mt_hbm, pi_hbm, out_hbm,
    xs, kg_src, mt, pi, hot, digit, tab, snd, rcv, kg_rcv, kap, gro, cellmap,
    fld0, fld1, edge, nothing, fsnd, frcv, basis, values, react, fin, fin_rcv, done_low,
    in_sem, a_send, a_recv, kg_send, kg_recv, h_send, h_recv, f_send, f_recv, out_sem,
):
    m, s = lax.axis_index("mode"), lax.axis_index("slab")
    depth = lax.axis_size("slab") // 4
    cx, ylo = m % 4, m // 4
    core, yhi, cz = s % 2, (s // 2) % 2, s // 4
    cy = yhi * 2 + ylo

    def at(x, y, z, c):
        return ((y % 2) * 4 + x, z * 4 + (y // 2) * 2 + c)

    loads = [pltpu.make_async_copy(x_hbm.at[p], xs.at[p], in_sem.at[p]) for p in range(3)]
    loads.append(pltpu.make_async_copy(dif_hbm, kg_src.at[0], in_sem.at[3]))
    loads.append(pltpu.make_async_copy(gro_hbm, kg_src.at[1], in_sem.at[4]))
    loads.append(pltpu.make_async_copy(mt_hbm, mt, in_sem.at[5]))
    loads.append(pltpu.make_async_copy(pi_hbm, pi, in_sem.at[6]))
    for c in loads:
        c.start()

    first_plane = jnp.logical_and(cz == 0, core == 0)
    last_plane = jnp.logical_and(cz == depth - 1, core == 1)
    up = at(cx, cy, jnp.minimum(cz + core, depth - 1), 1 - core)
    down = at(cx, cy, jnp.maximum(cz + core - 1, 0), 1 - core)
    partners = (
        at((cx + 1) % 4, cy, cz, core),
        at((cx + 3) % 4, cy, cz, core),
        at(cx, (cy + 1) % 4, cz, core),
        at(cx, (cy + 3) % 4, cz, core),
        up,
        down,
    )

    barrier = pltpu.get_barrier_semaphore()
    place = (cy * 4 + cx) * 2 + core

    def greet(k, carry):
        q = (place + k) % 32
        pl.semaphore_signal(
            barrier, inc=1, device_id=at((q // 2) % 4, q // 8, cz, q % 2), device_id_type=MESH
        )
        return carry

    lax.fori_loop(1, 32, greet, 0)

    @pl.when(jnp.logical_and(core == 1, cz < depth - 1))
    def _():
        pl.semaphore_signal(barrier, inc=1, device_id=up, device_id_type=MESH)

    @pl.when(jnp.logical_and(core == 0, cz > 0))
    def _():
        pl.semaphore_signal(barrier, inc=1, device_id=down, device_id_type=MESH)

    nothing[...] = jnp.zeros_like(nothing)

    for p in range(3):
        loads[p].wait()

    def spread(j, i):
        px, py = (cx + j) % 4, (cy + i) % 4
        return pltpu.make_async_remote_copy(
            src_ref=snd.at[py * 4 + px],
            dst_ref=rcv.at[m * 2 + core],
            send_sem=a_send.at[j * 4 + i],
            recv_sem=a_recv.at[m * 2 + core],
            device_id=at(px, py, cz, yhi),
            device_id_type=MESH,
        )

    own = pltpu.make_async_copy(snd.at[cy * 4 + cx], rcv.at[m * 2 + core], a_recv.at[m * 2 + core])

    def code_column(n):
        px = (cx + FAR[n]) % 4
        for p in range(3):
            for b in range(2):
                cols = pl.ds(pl.multiple_of(px * 256 + b * L, L), L)
                block = jnp.transpose(xs[p, :, cols])
                for y in range(4):
                    tile = jnp.concatenate(
                        [block[xi * 32 + y * 8 : xi * 32 + y * 8 + 8] for xi in range(4)], axis=0
                    )
                    row = p * 64 + b * 32
                    snd[y * 4 + px, row : row + 32, :] = tile

    def spread_column(n):
        j = FAR[n]
        for i in FAR:
            if i or j:
                spread(j, i).start()
            else:

                @pl.when(core == yhi)
                def _():
                    own.start()

                @pl.when(core != yhi)
                def _():
                    spread(0, 0).start()

    code_column(0)
    pl.semaphore_wait(
        barrier, 32 - jnp.logical_or(first_plane, last_plane).astype(I32)
    )
    spread_column(0)
    for n in range(1, 4):
        code_column(n)
        spread_column(n)

    loads[3].wait()
    loads[4].wait()

    def coeff(h):
        return pltpu.make_async_remote_copy(
            src_ref=kg_src,
            dst_ref=kg_rcv.at[core],
            send_sem=kg_send.at[h],
            recv_sem=kg_recv.at[core],
            device_id=(m, cz * 4 + h * 2 + yhi),
            device_id_type=MESH,
        )

    kg_own = pltpu.make_async_copy(kg_src, kg_rcv.at[core], kg_recv.at[core])

    @pl.when(core == yhi)
    def _():
        kg_own.start()
        coeff(1 - yhi).start()

    @pl.when(core != yhi)
    def _():
        coeff(yhi).start()
        coeff(1 - yhi).start()

    loads[5].wait()
    loads[6].wait()
    k8 = lax.broadcasted_iota(I32, (8, L), 0)
    power = jnp.where(
        k8 % 4 == 0, 1.0, jnp.where(k8 % 4 == 1, 3.0, jnp.where(k8 % 4 == 2, 9.0, 27.0))
    )
    degrees = mt[...].astype(F32).astype(BF16)
    pick_lane = lax.broadcasted_iota(I32, (MODES, L), 1)
    for j in range(2):
        weight = jnp.where(k8 // 4 == j, power, 0.0).astype(BF16)
        code_j = lax.dot_general(
            degrees, weight, (((0,), (0,)), ((), ())), preferred_element_type=F32
        ).astype(I32)
        for h in range(2):
            lane = pick_lane + h * L
            key = jnp.where(lane >= COMBOS, lane - COMBOS, lane)
            hot[j, :, h * L : (h + 1) * L] = jnp.where(key == code_j, 1.0, 0.0).astype(BF16)
    combo = lax.broadcasted_iota(I32, (COMBOS, 256), 0)
    for d in range(4):
        digit[d] = (combo // 3**d) % 3
        tab[:, 2 * COMBOS : 256, :] = jnp.zeros((2, 256 - 2 * COMBOS, 256), BF16)
    QB = 256

    def build(i, carry):
        cols = pl.ds(pl.multiple_of(i * QB, QB), QB)
        first = (pi[:, cols].astype(F32) - 3.0) * 0.32
        second = (first * first - 1.0) * 0.7071067811865476
        picked = []
        for j in range(2):
            for t in range(COMBOS // 16):
                halves = []
                for u in range(2):
                    r = t * 16 + u * 8
                    result = None
                    for d in range(4):
                        h1 = jnp.broadcast_to(first[j * 4 + d : j * 4 + d + 1], (8, QB))
                        h2 = jnp.broadcast_to(second[j * 4 + d : j * 4 + d + 1], (8, QB))
                        which = digit[d, r : r + 8, :]
                        factor = jnp.where(which == 0, 1.0, jnp.where(which == 1, h1, h2))
                        result = factor if result is None else result * factor
                    halves.append(result)
                both = jnp.concatenate(halves, axis=0)
                high = both.astype(BF16)
                tab[j, t * 16 : t * 16 + 16, :] = high
                tab[j, COMBOS + t * 16 : COMBOS + t * 16 + 16, :] = (
                    both - high.astype(F32)
                ).astype(BF16)
        for half in range(MODES // 256):
            rows = slice(half * 256, half * 256 + 256)
            picked = [
                jnp.dot(hot[j, rows, :], tab[j], preferred_element_type=F32) for j in range(2)
            ]
            basis[rows, cols] = (picked[0] * picked[1]).astype(BF16)
        return carry

    lax.fori_loop(0, POINTS // QB, build, 0)

    for c in range(2):
        pltpu.make_async_copy(kg_rcv.at[c], kg_rcv.at[c], kg_recv.at[c]).wait()
    for c in range(2):
        for b in range(2):
            cols = pl.ds(pl.multiple_of(cx * 256 + b * L, L), L)
            rows8 = [kg_rcv[c, 0, :, cols], kg_rcv[c, 1, :, cols], jnp.zeros((L - 6, L), F32)]
            cellmap[...] = jnp.transpose(jnp.concatenate(rows8, axis=0))
            for xi in range(4):
                tile = cellmap[pl.ds(pl.multiple_of(xi * 32 + cy * 8, 8), 8), :]
                for p in range(3):
                    to = (c * 3 + p) * 64 + (b * 4 + xi) * 8
                    kap[to : to + 8, :] = jnp.broadcast_to(tile[:, p : p + 1], (8, L))
                    gro[to : to + 8, :] = jnp.broadcast_to(tile[:, 3 + p : 4 + p], (8, L)) * 0.125

    def face_copy(sw, ch, f):
        rows = pl.ds(OFFS[f] * GPC, FACES[f] * GPC)
        return pltpu.make_async_remote_copy(
            src_ref=fsnd.at[sw, ch, rows],
            dst_ref=frcv.at[sw, ch, rows],
            send_sem=h_send.at[sw, max(f - 3, 0)],
            recv_sem=h_recv.at[sw, ch],
            device_id=partners[f],
            device_id_type=MESH,
        )

    def end_copy(sw, ch, f):
        rows = pl.ds(OFFS[f] * GPC, FACES[f] * GPC)
        return pltpu.make_async_copy(nothing, frcv.at[sw, ch, rows], h_recv.at[sw, ch])

    def send_faces(sw, fld, ch):
        for gg in range(GPC):
            g = ch * GPC + gg

            def put(f, value):
                row = OFFS[f] * GPC + gg * FACES[f]
                fsnd[sw, ch, row : row + FACES[f], :] = value

            put(0, jnp.concatenate([fld[g, z * 64 + 56 : z * 64 + 64, :] for z in range(6)], 0))
            put(1, jnp.concatenate([fld[g, z * 64 : z * 64 + 8, :] for z in range(6)], 0))
            put(2, jnp.concatenate([fld[g, pl.ds(z * 64 + 7, 8, stride=8), :] for z in range(6)], 0))
            put(3, jnp.concatenate([fld[g, pl.ds(z * 64, 8, stride=8), :] for z in range(6)], 0))
            put(4, fld[g, 320:384, :])
            put(5, fld[g, 0:64, :])

        for f in range(4):
            face_copy(sw, ch, f).start()

        @pl.when(jnp.logical_not(last_plane))
        def _():
            face_copy(sw, ch, 4).start()

        @pl.when(last_plane)
        def _():
            end_copy(sw, ch, 5).start()

        @pl.when(jnp.logical_not(first_plane))
        def _():
            face_copy(sw, ch, 5).start()

        @pl.when(first_plane)
        def _():
            end_copy(sw, ch, 4).start()

    sub = lax.broadcasted_iota(I32, (8, L), 0)

    def sweep(sw, old, new, ch):
        pltpu.make_async_copy(frcv.at[sw, ch], frcv.at[sw, ch], h_recv.at[sw, ch]).wait()
        for gg in range(GPC):
            g = ch * GPC + gg

            def halo(f):
                row = OFFS[f] * GPC + gg * FACES[f]
                return frcv[sw, ch, row : row + FACES[f], :]

            xl, xh, yl, yh, zl, zh = [halo(f) for f in range(6)]
            for z in range(6):
                edge[gg, pl.ds(z * 64, 8, stride=8), :] = yl[z * 8 : z * 8 + 8]
                edge[gg, pl.ds(z * 64 + 7, 8, stride=8), :] = yh[z * 8 : z * 8 + 8]
            for z in range(6):
                for x in range(8):
                    r = z * 64 + x * 8
                    mid = old[g, r : r + 8, :]
                    xm = old[g, r - 8 : r, :] if x else xl[z * 8 : z * 8 + 8]
                    xp = old[g, r + 8 : r + 16, :] if x < 7 else xh[z * 8 : z * 8 + 8]
                    zm = old[g, r - 64 : r - 56, :] if z else zl[x * 8 : x * 8 + 8]
                    zp = old[g, r + 64 : r + 72, :] if z < 5 else zh[x * 8 : x * 8 + 8]
                    ends = edge[gg, r : r + 8, :]
                    ym = jnp.where(sub == 0, ends, pltpu.roll(mid, 1, 0))
                    yp = jnp.where(sub == 7, ends, pltpu.roll(mid, 7, 0))
                    total = ((xm + xp) + (ym + yp)) + (zp + zm)
                    new[g, r : r + 8, :] = mid + kap[r : r + 8, :] * (total - 6.0 * mid)

    QC = 256

    def forward(fld, ch):
        part = jnp.concatenate([fld[ch * GPC + gg, 0:ROWS, :].astype(BF16) for gg in range(GPC)], axis=1)
        rows = slice(ch * GPC * L, (ch + 1) * GPC * L)
        for i in range(POINTS // QC):
            at_q = slice(i * QC, (i + 1) * QC)
            v = jnp.dot(part, basis[rows, at_q], preferred_element_type=F32)
            if ch:
                v = values[:, at_q] + v
            if ch < NCH - 1:
                values[:, at_q] = v
            else:
                rate = jnp.concatenate([gro[...]] * (QC // L), axis=1)
                react[:, at_q] = (v * (rate - (v * v) * (1.0 / 128.0))).astype(BF16)

    def diffuse(first_sweep, here, there):
        for t in range(SWEEPS - 1):
            sw = first_sweep + t

            def one(ch, carry, sw=sw, here=here, there=there):
                sweep(sw, here, there, ch)
                send_faces(sw + 1, there, ch)
                return carry

            lax.fori_loop(0, NCH, one, 0)
            here, there = there, here
        for ch in range(NCH):
            sweep(first_sweep + SWEEPS - 1, here, there, ch)
            forward(there, ch)

    def increment(ch):
        cols = slice(ch * GPC * L, (ch + 1) * GPC * L)
        inc = lax.dot_general(
            react[...], basis[cols, :], (((1,), (1,)), ((), ())), preferred_element_type=F32
        )
        return inc * (1.4 * MODES**0.5 / POINTS)

    def arrive(ch, carry):
        def one(gg, carry):
            g = ch * GPC + gg
            for c in range(2):
                slot = g * 2 + c
                pltpu.make_async_copy(rcv.at[slot], rcv.at[slot], a_recv.at[slot]).wait()
                fld0[g, c * HALF : (c + 1) * HALF, :] = rcv[slot]
            return carry

        lax.fori_loop(0, GPC, one, 0)
        send_faces(0, fld0, ch)
        return carry

    lax.fori_loop(0, NCH, arrive, 0)

    diffuse(0, fld0, fld1)
    for ch in range(NCH):
        inc = increment(ch)
        for gg in range(GPC):
            fld1[ch * GPC + gg, 0:ROWS, :] += inc[:, gg * L : (gg + 1) * L]
        send_faces(SWEEPS, fld1, ch)
    diffuse(SWEEPS, fld1, fld0)

    patch = cy * 4 + cx

    def home(g, c):
        return pltpu.make_async_remote_copy(
            src_ref=fin.at[g * 2 + c],
            dst_ref=fin_rcv.at[patch],
            send_sem=f_send.at[g * 2 + c],
            recv_sem=f_recv.at[patch],
            device_id=(g, cz * 4 + core * 2 + c),
            device_id_type=MESH,
        )

    def stays(g, c):
        return pltpu.make_async_copy(fin.at[g * 2 + c], fin_rcv.at[patch], f_recv.at[patch])

    def is_own(g, c):
        return jnp.logical_and(g == m, jnp.logical_and(core == yhi, c == core))

    for ch in range(NCH):
        inc = increment(ch)
        for gg in range(GPC):
            g = ch * GPC + gg
            done = (fld0[g, 0:ROWS, :] + inc[:, gg * L : (gg + 1) * L]).astype(BF16)
            for c in range(2):
                fin[g * 2 + c] = done[c * HALF : (c + 1) * HALF]

                @pl.when(is_own(g, c))
                def _():
                    stays(g, c).start()

                @pl.when(jnp.logical_not(is_own(g, c)))
                def _():
                    home(g, c).start()


    @pl.when(core != yhi)
    def _():
        spread(0, 0).wait_send()
        coeff(yhi).wait_send()
        coeff(1 - yhi).wait_send()

    @pl.when(core == yhi)
    def _():
        coeff(1 - yhi).wait_send()

    def spread_done(k, carry):
        spread(k // 4, k % 4).wait_send()
        return carry

    lax.fori_loop(1, 16, spread_done, 0)

    def faces_done(sw, carry):
        def sent(f, lo, hi):
            part = fsnd.at[sw, :, pl.ds(lo * GPC, (hi - lo) * GPC)]
            pltpu.make_async_copy(part, part, h_send.at[sw, f]).wait()

        sent(0, 0, 192)

        @pl.when(jnp.logical_not(last_plane))
        def _():
            sent(1, 192, 256)

        @pl.when(jnp.logical_not(first_plane))
        def _():
            sent(2, 256, 320)

        return carry

    lax.fori_loop(0, 2 * SWEEPS, faces_done, 0)

    def out_copy(px):
        cols = pl.ds(pl.multiple_of(px * 256, 256), 256)
        return pltpu.make_async_copy(
            done_low.at[:, :, cols], out_hbm.at[:, :, cols], out_sem.at[px]
        )

    def collect(j, carry):
        px = (cx + j + (j // 2) * (5 - 2 * j)) % 4
        for y in range(4):
            slot = y * 4 + px
            pltpu.make_async_copy(fin_rcv.at[slot], fin_rcv.at[slot], f_recv.at[slot]).wait()
        for p in range(3):
            for b in range(2):
                row = p * 64 + b * 32
                parts = [fin_rcv[y * 4 + px, row : row + 32, :].astype(F32) for y in range(4)]
                block = jnp.concatenate(
                    [parts[y][xi * 8 : xi * 8 + 8] for xi in range(4) for y in range(4)], axis=0
                )
                cols = pl.ds(pl.multiple_of(px * 256 + b * L, L), L)
                done_low[p, :, cols] = jnp.transpose(block).astype(BF16)
        out_copy(px).start()
        return carry

    lax.fori_loop(0, 4, collect, 0)

    def home_done(i, carry):
        g, c = i // 2, i % 2

        @pl.when(jnp.logical_not(is_own(g, c)))
        def _():
            home(g, c).wait_send()

        return carry

    lax.fori_loop(0, 16, home_done, 0)
    for px in range(4):
        out_copy(px).wait()


def per_device(chaos_field, diffusivity, growth_rate, mode_table, point_index):
    any_spec = pl.BlockSpec(memory_space=pl.ANY)
    V = pltpu.VMEM
    DMA = pltpu.SemaphoreType.DMA
    planes_first = jnp.transpose(chaos_field, (1, 0, 2))
    result = pl.pallas_call(
        kernel,
        out_shape=jax.ShapeDtypeStruct(planes_first.shape, BF16),
        in_specs=[any_spec] * 5,
        out_specs=any_spec,
        scratch_shapes=[
            V((3, L, 1024), F32),
            V((2, 3, 1024), F32),
            V((8, MODES), I32),
            V((8, POINTS), I32),
            V((2, MODES, 256), BF16),
            V((4, COMBOS, 256), I32),
            V((2, 256, 256), BF16),
            V((16, HALF, L), F32),
            V((16, HALF, L), F32),
            V((2, 2, 3, 1024), F32),
            V((ROWS, L), F32),
            V((ROWS, L), F32),
            V((L, L), F32),
            V((GROUPS, ROWS + 8, L), F32),
            V((GROUPS, ROWS + 8, L), F32),
            V((GPC, ROWS + 8, L), F32),
            V((64 * GPC, L), F32),
            V((2 * SWEEPS, NCH, FROWS * GPC, L), F32),
            V((2 * SWEEPS, NCH, FROWS * GPC, L), F32),
            V((MODES, POINTS), BF16),
            V((ROWS, POINTS), F32),
            V((ROWS, POINTS), BF16),
            V((16, HALF, L), BF16),
            V((16, HALF, L), BF16),
            V((3, L, 1024), BF16),
            DMA((7,)),
            DMA((16,)),
            DMA((16,)),
            DMA((2,)),
            DMA((2,)),
            DMA((2 * SWEEPS, 3)),
            DMA((2 * SWEEPS, NCH)),
            DMA((16,)),
            DMA((16,)),
            DMA((4,)),
        ],
        compiler_params=pltpu.CompilerParams(
            collective_id=0, has_side_effects=True, vmem_limit_bytes=58 * 1024 * 1024
        ),
    )(planes_first, diffusivity, growth_rate, mode_table.T, point_index.T)
    return jnp.transpose(result.astype(F32), (1, 0, 2))


def solution(mesh):
    return jax.shard_map(
        per_device,
        mesh=mesh,
        in_specs=(P("mode", "slab", None), P("slab", None), P("slab", None), P(), P()),
        out_specs=P("mode", "slab", None),
        check_vma=False,
    )
```
